128 devices in a mesh: freq: 32 (over y, x, core), tm: 4 (over z).
Axes of the slice: x: 4, y: 4, z: 4, core: 2. Of those that a mesh axis runs over, the one named last changes fastest.
Arguments:
- voltages: bfloat16 [2, 1024, 128, 1024], P(None, 'tm', 'freq'), may hold values from -6 to 6
- gains: float32 [2, 128, 1024], P(None, 'freq'), may hold values from -5 to 5
- window: float32 [64], replicated, may hold values from 0.2 to 1
Outputs:
- intensity: float32 [1024, 16, 2048], P('freq', 'tm')
The draws below stay inside these ranges and needn't reach their ends.
All inputs are finite; a program needn't handle non-finite values.
Results may differ from the reference program's by a relative error of at most 0.0065.
Values may be sent and summed in bfloat16 or wider, within the bound.
No kernel may reach another device: no remote copies, remote signals or barrier semaphores. Data moves between devices by JAX's collectives and lax.ppermute only.
A program may use at most 128 MiB of HBM per device.

```python
import math
import jax
import jax.numpy as jnp
from jax import lax

EW = 4
NS = 256
FEEDS = 1024
FINE = 16
TAPS = 4
INTEG = 4
CHAN = 128
SAMPLES = 1024
OUT_T = 16


def block_levels(stream_key, dims, pieces, least, largest):
    factor_of, own = 1.0, jax.random.fold_in(stream_key, 6)
    for axis_at, parts in pieces:
        heights = jnp.exp(jax.random.uniform(jax.random.fold_in(own, axis_at), (parts,), jnp.float32, least / len(pieces), largest / len(pieces)))
        factor_of = factor_of * jnp.repeat(heights, dims[axis_at] // parts).reshape([-1 if axis == axis_at else 1 for axis in range(len(dims))])
    return factor_of


def normal_values(key, shape, scale, most, cuts=(), kind=jnp.bfloat16):
    array = jax.random.normal(key, shape, jnp.float32) * scale
    if len(cuts) > 0:
        array = block_levels(key, shape, cuts, -0.22, 0.18) * array
    return jnp.clip(array, min=-most, max=most).astype(kind)


def setup_inputs(seed: int = 0) -> dict:
    streams_of = jax.random.split(jax.random.key(seed), 4)
    return {
        "voltages": normal_values(streams_of[0], (2, SAMPLES, CHAN, FEEDS), 1.0, 6.0, ((1, 4), (2, 32))),
        "gains": normal_values(streams_of[1], (2, CHAN, FEEDS), 1.0, 5.0, ((1, 32),), jnp.float32),
        "window": jnp.clip(jax.random.uniform(streams_of[2], (TAPS * FINE,), jnp.float32, 0.2, 1.0), 0.2, 1.0),
    }


def fourier_tables(count):
    indices = jnp.arange(count, dtype=jnp.int32)
    products = indices[:, None] * indices[None, :] % count
    angles = products.astype(jnp.float32) * (2.0 * math.pi / count)
    return (jnp.cos(angles), jnp.sin(angles))

def channel_power(samples, gain_pair, window, cos_ns, sin_ns, cos_ew, sin_ew):
    frame_count = SAMPLES // FINE
    zeros_head = jnp.zeros((2, (TAPS - 1) * FINE, FEEDS), samples.dtype)
    extended = jnp.concatenate([zeros_head, samples], axis=1).astype(jnp.float32)
    extended = extended.reshape(2, frame_count + TAPS - 1, FINE, FEEDS)
    tap_rows = window.reshape(TAPS, FINE)
    tapped = jnp.zeros((2, frame_count, FINE, FEEDS), jnp.float32)
    for m_tap in range(TAPS):
        start = TAPS - 1 - m_tap
        tapped = tapped + tap_rows[m_tap][None, None, :, None] * extended[:, start:start + frame_count]
    tapped = tapped * (1.0 / math.sqrt(FINE * TAPS))
    cos_fine, sin_fine = fourier_tables(FINE)
    high = lax.Precision.HIGHEST
    spec_real = jnp.einsum('fn,jnp->jfp', cos_fine, tapped[0], precision=high) + jnp.einsum('fn,jnp->jfp', sin_fine, tapped[1], precision=high)
    spec_imag = jnp.einsum('fn,jnp->jfp', cos_fine, tapped[1], precision=high) - jnp.einsum('fn,jnp->jfp', sin_fine, tapped[0], precision=high)
    gain_real = gain_pair[0][None, None, :]
    gain_imag = gain_pair[1][None, None, :]
    row_count = frame_count * FINE
    cal_real = (gain_real * spec_real - gain_imag * spec_imag).astype(jnp.bfloat16)
    cal_imag = (gain_real * spec_imag + gain_imag * spec_real).astype(jnp.bfloat16)
    cal_real = cal_real.astype(jnp.float32).reshape(row_count, EW, NS)
    cal_imag = cal_imag.astype(jnp.float32).reshape(row_count, EW, NS)
    scale_ns = 1.0 / math.sqrt(NS)
    part_real = (jnp.einsum('xen,kn->xek', cal_real, cos_ns, precision=high) + jnp.einsum('xen,kn->xek', cal_imag, sin_ns, precision=high)) * scale_ns
    part_imag = (jnp.einsum('xen,kn->xek', cal_imag, cos_ns, precision=high) - jnp.einsum('xen,kn->xek', cal_real, sin_ns, precision=high)) * scale_ns
    part_real = part_real.astype(jnp.bfloat16).astype(jnp.float32)
    part_imag = part_imag.astype(jnp.bfloat16).astype(jnp.float32)
    scale_ew = 1.0 / math.sqrt(EW)
    beam_real = (jnp.einsum('ge,xek->gkx', cos_ew, part_real, precision=high) + jnp.einsum('ge,xek->gkx', sin_ew, part_imag, precision=high)) * scale_ew
    beam_imag = (jnp.einsum('ge,xek->gkx', cos_ew, part_imag, precision=high) - jnp.einsum('ge,xek->gkx', sin_ew, part_real, precision=high)) * scale_ew
    beam_real = beam_real.astype(jnp.bfloat16).astype(jnp.float32)
    beam_imag = beam_imag.astype(jnp.bfloat16).astype(jnp.float32)
    detected = beam_real * beam_real + beam_imag * beam_imag
    detected = detected.reshape(FEEDS, OUT_T, INTEG, FINE)
    return lax.optimization_barrier(jnp.mean(detected, axis=2))

def reference(voltages, gains, window):
    cos_ns, sin_ns = fourier_tables(NS)
    cos_ns = cos_ns.astype(jnp.bfloat16).astype(jnp.float32)
    sin_ns = sin_ns.astype(jnp.bfloat16).astype(jnp.float32)
    cos_ew, sin_ew = fourier_tables(EW)
    cos_ew = cos_ew.astype(jnp.bfloat16).astype(jnp.float32)
    sin_ew = sin_ew.astype(jnp.bfloat16).astype(jnp.float32)

    def one_channel(channel):
        samples = lax.dynamic_index_in_dim(voltages, channel, 2, keepdims=False)
        gain_pair = lax.dynamic_index_in_dim(gains, channel, 1, keepdims=False)
        return channel_power(samples, gain_pair, window, cos_ns, sin_ns, cos_ew, sin_ew)
    stacked = lax.map(one_channel, jnp.arange(CHAN, dtype=jnp.int32))
    stacked = jnp.transpose(stacked, (1, 2, 0, 3))
    return stacked.reshape(FEEDS, OUT_T, CHAN * FINE)
```

```python
import math

import jax
import jax.numpy as jnp
import numpy as np
from jax import lax
from jax.experimental import pallas as pl
from jax.experimental.pallas import tpu as pltpu
from jax.sharding import PartitionSpec as P

EW = 4
NS = 256
FEEDS = EW * NS
FINE = 16
TAPS = 4
INTEG = 4
CHAN = 4
SPAN = INTEG * FINE
PAST = (TAPS - 1) * FINE
GROUP = 32
HALF = 16
TIMES = 4

F32 = jnp.float32
BF16 = jnp.bfloat16


def fine_tables():
    f = np.arange(FINE)[:, None]
    n = np.arange(2 * SPAN)[None, :] % FINE
    angle = (f * n % FINE) * (2.0 * math.pi / FINE)
    scale = 1.0 / math.sqrt(FINE * TAPS)
    return np.stack([np.cos(angle), np.sin(angle)]).astype(np.float32) * np.float32(scale)


def beam_table():
    q = np.arange(NS)[:, None]
    lane = np.arange(NS)[None, :]
    k = (lane % 128) // HALF * GROUP + lane // 128 * HALF + lane % HALF
    angle = (q * k % NS).astype(np.float32) * np.float32(2.0 * math.pi / NS)
    cos = np.cos(angle).astype(jnp.bfloat16).astype(np.float32)
    sin = np.sin(angle).astype(jnp.bfloat16).astype(np.float32)
    scale = 1.0 / math.sqrt(NS) / math.sqrt(EW) / math.sqrt(INTEG)
    table = np.block([[cos, -sin], [sin, cos]]) * np.float32(scale)
    return table.astype(jnp.bfloat16)


def fill_bank(window_ref, fine_ref, bank_ref):
    taps = jnp.concatenate([window_ref[...], jnp.zeros((1, 64), F32)], axis=1)
    lane = lax.broadcasted_iota(jnp.int32, (1, 2 * SPAN), 1)
    line = jnp.zeros((1, 2 * SPAN), F32)
    for m in range(TAPS):
        moved = pltpu.roll(taps, (64 - 32 * m) % 128, 1)
        line = jnp.where(lane // FINE == TAPS - m, moved, line)
    cos, sin = fine_ref[0], fine_ref[1]
    for j in range(INTEG):
        row = line if j == 0 else pltpu.roll(line, FINE * j, 1)
        re, im = (cos * row).astype(BF16), (sin * row).astype(BF16)
        bank_ref[FINE * j : FINE * (j + 1), :128] = re
        bank_ref[FINE * j : FINE * (j + 1), 128:] = im
        bank_ref[64 + FINE * j : 64 + FINE * (j + 1), :128] = -im
        bank_ref[64 + FINE * j : 64 + FINE * (j + 1), 128:] = re


def form_time(now, past_of, gains_ref, table_ref, bank_ref, left_ref, out_ref):
    for c in range(CHAN):
        data = jnp.concatenate(
            [past_of(0, c), now[0][c], past_of(1, c), now[1][c]], axis=0
        )
        spec = jnp.dot(bank_ref[...], data, preferred_element_type=F32)
        sr, si = spec[:SPAN], spec[SPAN:]
        gr, gi = gains_ref[0, c : c + 1], gains_ref[1, c : c + 1]
        cr = gr * sr - gi * si
        ci = gr * si + gi * sr
        r0, r1, r2, r3 = (cr[:, NS * e : NS * (e + 1)] for e in range(EW))
        i0, i1, i2, i3 = (ci[:, NS * e : NS * (e + 1)] for e in range(EW))
        rs, rd, it, iu = r0 + r2, r0 - r2, i0 + i2, i0 - i2
        rv, rw, iv, iw = r1 + r3, r1 - r3, i1 + i3, i1 - i3
        beams = ((rs + rv, it + iv), (rd + iw, iu - rw), (rs - rv, it - iv), (rd - iw, iu + rw))
        for g in range(EW):
            re, im = beams[g][0].astype(BF16), beams[g][1].astype(BF16)
            for j in range(INTEG):
                at = 256 * g + 64 * j + FINE * c
                left_ref[at : at + FINE, :NS] = re[FINE * j : FINE * (j + 1)]
                left_ref[at : at + FINE, NS:] = im[FINE * j : FINE * (j + 1)]
    for g in range(EW):
        beam = jnp.dot(
            left_ref[256 * g : 256 * (g + 1)], table_ref[...], preferred_element_type=F32
        )
        re, im = beam[:, :NS], beam[:, NS:]
        power = re * re + im * im
        power = power[:64] + power[64:128] + power[128:192] + power[192:]
        power = jnp.concatenate([power[:, :128], power[:, 128:]], axis=0)
        out_ref[8 * g : 8 * (g + 1)] = power.T.astype(BF16).reshape(8, HALF, 128)


def later_kernel(volt_ref, gains_ref, window_ref, fine_ref, table_ref, out_ref, bank_ref, kept_ref, left_ref):
    step = pl.program_id(0)

    @pl.when(step == 0)
    def _():
        fill_bank(window_ref, fine_ref, bank_ref)
        for part in range(2):
            kept_ref[part] = jnp.swapaxes(volt_ref[part], 0, 1)

    @pl.when(step > 0)
    def _():
        now = [jnp.swapaxes(volt_ref[part], 0, 1) for part in range(2)]
        form_time(now, lambda part, c: kept_ref[part, c], gains_ref, table_ref, bank_ref, left_ref, out_ref)
        for part in range(2):
            kept_ref[part] = now[part]


def first_kernel(volt_ref, halo_ref, gains_ref, window_ref, fine_ref, table_ref, rest_ref, out_ref, bank_ref, left_ref):
    fill_bank(window_ref, fine_ref, bank_ref)
    now = [jnp.swapaxes(volt_ref[part], 0, 1) for part in range(2)]
    past = [jnp.swapaxes(halo_ref[part], 0, 1) for part in range(2)]
    zeros = jnp.zeros((SPAN - PAST, FEEDS), BF16)
    form_time(
        now, lambda part, c: jnp.concatenate([zeros, past[part][c]], axis=0),
        gains_ref, table_ref, bank_ref, left_ref, out_ref,
    )


def join_kernel(got_ref, out_ref):
    lane = lax.broadcasted_iota(jnp.int32, (1, 128), 1)
    low = lane < 64
    for s in range(GROUP // 2):
        a = got_ref[2 * s].astype(F32)
        b = got_ref[2 * s + 1].astype(F32)
        first = jnp.where(low, a, pltpu.roll(b, 64, 1)).reshape(TIMES, HALF, 128)
        second = jnp.where(low, pltpu.roll(a, 64, 1), b).reshape(TIMES, HALF, 128)
        out_ref[:HALF, :, 128 * s : 128 * (s + 1)] = jnp.swapaxes(first, 0, 1)
        out_ref[HALF:, :, 128 * s : 128 * (s + 1)] = jnp.swapaxes(second, 0, 1)


PARAMS = pltpu.CompilerParams(vmem_limit_bytes=48 << 20)


def whole(*shape):
    return pl.BlockSpec(shape, lambda *_: (0,) * len(shape))


def body(voltages, gains, window):
    samples = voltages.shape[1]
    halo = voltages[:, samples - PAST :]
    count = lax.axis_size("tm")
    halo = lax.ppermute(halo, "tm", [(i, i + 1) for i in range(count - 1)])
    fine = jnp.asarray(fine_tables())
    table = jnp.asarray(beam_table())
    window = window.reshape(1, FINE * TAPS)
    shape = jax.ShapeDtypeStruct((GROUP, TIMES * HALF, 128), BF16)
    shared = [
        whole(2, CHAN, FEEDS), whole(1, FINE * TAPS), whole(2, FINE, 2 * SPAN), whole(2 * NS, 2 * NS)
    ]
    flops = 2 * (4 * 128 * 256 * 1024 + 1024 * 512 * 512)
    rest = pl.pallas_call(
        later_kernel,
        grid=(TIMES,),
        in_specs=[pl.BlockSpec((2, SPAN, CHAN, FEEDS), lambda t: (0, t, 0, 0))] + shared,
        out_specs=pl.BlockSpec((GROUP, HALF, 128), lambda t: (0, jnp.maximum(t, 1), 0)),
        out_shape=shape,
        scratch_shapes=[
            pltpu.VMEM((128, 256), BF16),
            pltpu.VMEM((2, CHAN, SPAN, FEEDS), BF16),
            pltpu.VMEM((1024, 512), BF16),
        ],
        compiler_params=PARAMS,
        cost_estimate=pl.CostEstimate(flops=3 * flops, bytes_accessed=5 << 20, transcendentals=0),
        name="later_times",
    )(voltages, gains, window, fine, table)
    power = pl.pallas_call(
        first_kernel,
        grid=(1,),
        in_specs=[
            pl.BlockSpec((2, SPAN, CHAN, FEEDS), lambda t: (0, 0, 0, 0)),
            whole(2, PAST, CHAN, FEEDS),
        ] + shared + [pl.BlockSpec(memory_space=pl.ANY)],
        out_specs=pl.BlockSpec((GROUP, HALF, 128), lambda t: (0, 0, 0)),
        out_shape=shape,
        scratch_shapes=[pltpu.VMEM((128, 256), BF16), pltpu.VMEM((1024, 512), BF16)],
        input_output_aliases={6: 0},
        compiler_params=PARAMS,
        cost_estimate=pl.CostEstimate(flops=flops, bytes_accessed=3 << 20, transcendentals=0),
        name="first_time",
    )(voltages, halo, gains, window, fine, table, rest)
    got = lax.all_to_all(power, "freq", split_axis=0, concat_axis=0, tiled=True)
    return pl.pallas_call(
        join_kernel,
        out_shape=jax.ShapeDtypeStruct((GROUP, TIMES, GROUP * CHAN * FINE), F32),
        compiler_params=PARAMS,
        name="join_channels",
    )(got)


def solution(mesh):
    placed = (P(None, "tm", "freq", None), P(None, "freq", None), P())
    return jax.shard_map(
        body, mesh=mesh, in_specs=placed, out_specs=P("freq", "tm", None), check_vma=False
    )
```

```python
import math

import jax
import jax.numpy as jnp
import numpy as np
from jax import lax
from jax.experimental import pallas as pl
from jax.experimental.pallas import tpu as pltpu
from jax.sharding import PartitionSpec as P

EW = 4
NS = 256
FEEDS = EW * NS
FINE = 16
TAPS = 4
INTEG = 4
CHAN = 4
AHEAD = 3
SPAN = INTEG * FINE
PAST = (TAPS - 1) * FINE
GROUP = 32
HALF = 16
TIMES = 4
EARLY = TAPS - 1

F32 = jnp.float32
BF16 = jnp.bfloat16


def beam_table():
    q = np.arange(NS // 2)[:, None]
    tables = []
    scale = 1.0 / math.sqrt(NS) / math.sqrt(EW) / math.sqrt(INTEG)
    for odd in range(2):
        k = 2 * np.arange(NS // 2)[None, :] + odd
        angle = (q * k % NS).astype(np.float32) * np.float32(2.0 * math.pi / NS)
        cos = np.cos(angle).astype(jnp.bfloat16).astype(np.float32)
        sin = np.sin(angle).astype(jnp.bfloat16).astype(np.float32)
        tables.append(np.block([[cos, -sin], [sin, cos]]) * np.float32(scale))
    return np.stack(tables).astype(jnp.bfloat16)


def fill_bank(window_ref, bank_ref):
    taps = jnp.concatenate([window_ref[...], jnp.zeros((1, 64), F32)], axis=1)
    lane = lax.broadcasted_iota(jnp.int32, (1, 2 * SPAN), 1)
    line = jnp.zeros((1, 2 * SPAN), F32)
    for m in range(TAPS):
        moved = pltpu.roll(taps, (64 - 32 * m) % 128, 1)
        line = jnp.where(lane // FINE == TAPS - m, moved, line)
    f = lax.broadcasted_iota(jnp.int32, (FINE, 2 * SPAN), 0)
    n = lax.broadcasted_iota(jnp.int32, (FINE, 2 * SPAN), 1) % FINE
    turn = f * n % FINE
    scale = 1.0 / math.sqrt(FINE * TAPS)
    cos = jnp.zeros((FINE, 2 * SPAN), F32)
    sin = jnp.zeros((FINE, 2 * SPAN), F32)
    for k in range(FINE):
        angle = 2.0 * math.pi * k / FINE
        cos = jnp.where(turn == k, scale * math.cos(angle), cos)
        sin = jnp.where(turn == k, scale * math.sin(angle), sin)
    for j in range(INTEG):
        row = line if j == 0 else pltpu.roll(line, FINE * j, 1)
        re, im = (cos * row).astype(BF16), (sin * row).astype(BF16)
        bank_ref[FINE * j : FINE * (j + 1), :128] = re
        bank_ref[FINE * j : FINE * (j + 1), 128:] = im
        bank_ref[64 + FINE * j : 64 + FINE * (j + 1), :128] = -im
        bank_ref[64 + FINE * j : 64 + FINE * (j + 1), 128:] = re


def steer(spec, gr, gi):
    half = spec.shape[0] // 2
    sr, si = spec[:half], spec[half:]
    cr = gr * sr - gi * si
    ci = gr * si + gi * sr
    r0, r1, r2, r3 = (cr[:, NS * e : NS * (e + 1)] for e in range(EW))
    i0, i1, i2, i3 = (ci[:, NS * e : NS * (e + 1)] for e in range(EW))
    rs, rd, it, iu = r0 + r2, r0 - r2, i0 + i2, i0 - i2
    rv, rw, iv, iw = r1 + r3, r1 - r3, i1 + i3, i1 - i3
    return (rs + rv, it + iv), (rd + iw, iu - rw), (rs - rv, it - iv), (rd - iw, iu + rw)


def powers(bank, data_of, channels, frames, gains_ref, table_ref, left_ref):
    count = len(channels)
    rows = frames * count * FINE
    for at, c in enumerate(channels):
        spec = jnp.dot(bank, data_of(c), preferred_element_type=F32)
        beams = steer(spec, gains_ref[0, c : c + 1], gains_ref[1, c : c + 1])
        for g in range(EW):
            for part in range(2):
                low, high = beams[g][part][:, :128], beams[g][part][:, 128:]
                for odd, value in enumerate((low + high, low - high)):
                    value = value.astype(BF16)
                    lane = 256 * odd + 128 * part
                    for j in range(frames):
                        row = rows * g + FINE * (count * j + at)
                        left_ref[row : row + FINE, lane : lane + 128] = value[FINE * j : FINE * (j + 1)]
    part = rows // frames
    sums = []
    for g in range(EW):
        both = []
        for odd in range(2):
            beam = jnp.dot(
                left_ref[rows * g : rows * (g + 1), 256 * odd : 256 * (odd + 1)],
                table_ref[odd], preferred_element_type=F32,
            )
            re, im = beam[:, :128], beam[:, 128:]
            power = re * re + im * im
            total = power[:part]
            for j in range(1, frames):
                total = total + power[part * j : part * (j + 1)]
            both.append(total)
        sums.append(both)
    return sums


def by_beam(even, odd):
    power = jnp.concatenate([even, odd], axis=0)
    return power.T.astype(BF16).reshape(8, HALF, 128)


def early_bank(bank_ref):
    return jnp.concatenate([bank_ref[: FINE * EARLY], bank_ref[64 : 64 + FINE * EARLY]], axis=0)


def edge_copies(volt_ref, start, to_ref, sems):
    return [
        pltpu.make_async_copy(volt_ref.at[part, pl.ds(start, PAST)], to_ref.at[part], sems.at[part])
        for part in range(2)
    ]


def tail_kernel(volt_ref, ahead_ref, keep_ref, tail_ref, sems):
    copies = edge_copies(volt_ref, volt_ref.shape[1] - PAST, tail_ref, sems)
    for copy in copies:
        copy.start()
    for part in range(2):
        copies[part].wait()
        tail = jnp.swapaxes(tail_ref[part], 0, 1)
        ahead_ref[part] = tail[:AHEAD]
        keep_ref[part] = tail[AHEAD]


def head_kernel(volt_ref, back_ref, first_ref, head_ref, sems):
    copies = [
        pltpu.make_async_copy(volt_ref.at[part, pl.ds(0, SPAN)], head_ref.at[part], sems.at[part])
        for part in range(2)
    ]
    for copy in copies:
        copy.start()
    for part in range(2):
        copies[part].wait()
        head = jnp.swapaxes(head_ref[part], 0, 1)
        first_ref[part] = head
        back_ref[part] = head[AHEAD, :PAST]


def form_time(t, past, now_ref, gains_ref, table_ref, bank_ref, out_ref, left_ref):
    now = [jnp.swapaxes(now_ref[part], 0, 1) for part in range(2)]
    sums = powers(
        bank_ref[...],
        lambda c: jnp.concatenate([past[0][c], now[0][c], past[1][c], now[1][c]], axis=0),
        range(CHAN), INTEG, gains_ref, table_ref, left_ref,
    )
    for g in range(EW):
        out_ref[8 * g : 8 * (g + 1), HALF * t : HALF * (t + 1)] = by_beam(*sums[g])
    return now


def second_kernel(
    volt_ref, first_ref, gains_ref, table_ref, window_ref,
    out_ref, bank_ref, late_ref, second_ref, ahead_ref, block_ref, left_ref, sems,
):
    to = [block_ref] + [ahead_ref.at[i] for i in range(TIMES - 2)]
    copies = [
        pltpu.make_async_copy(volt_ref.at[:, pl.ds(SPAN * (i + 1), SPAN)], to[i], sems.at[i])
        for i in range(TIMES - 1)
    ]
    for copy in copies:
        copy.start()
    fill_bank(window_ref, bank_ref)
    sums = powers(
        jnp.concatenate([bank_ref[48:64], bank_ref[112:128]], axis=0),
        lambda c: jnp.concatenate([first_ref[0, c], first_ref[0, c], first_ref[1, c], first_ref[1, c]], axis=0),
        range(CHAN), 1, gains_ref, table_ref, left_ref,
    )
    for g in range(EW):
        for odd in range(2):
            late_ref[g, odd] = sums[g][odd]
    copies[0].wait()
    now = form_time(1, first_ref, block_ref, gains_ref, table_ref, bank_ref, out_ref, left_ref)
    for part in range(2):
        second_ref[part] = now[part]
    for copy in copies[1:]:
        copy.wait()


def later_kernel(ahead_ref, second_ref, gains_ref, table_ref, bank_ref, rest_ref, out_ref, left_ref):
    now = form_time(2, second_ref, ahead_ref.at[0], gains_ref, table_ref, bank_ref, out_ref, left_ref)
    form_time(3, now, ahead_ref.at[1], gains_ref, table_ref, bank_ref, out_ref, left_ref)


def neighbour_kernel(head_ref, keep_ref, gains_ref, table_ref, bank_ref, out_ref, left_ref):
    last = lax.axis_index("tm") == lax.axis_size("tm") - 1
    bank = early_bank(bank_ref)
    lane = lax.broadcasted_iota(jnp.int32, bank.shape, 1)
    edge = jnp.where(last, SPAN, 0)
    bank = jnp.where(lane % 128 < edge, 0.0, bank.astype(F32)).astype(BF16)
    pad = jnp.zeros((SPAN - PAST, FEEDS), BF16)
    sums = powers(
        bank,
        lambda c: jnp.concatenate(
            [pad, keep_ref[0], head_ref[0], pad, pad, keep_ref[1], head_ref[1], pad], axis=0
        ),
        (AHEAD,), EARLY, gains_ref, table_ref, left_ref,
    )
    for g in range(EW):
        for odd in range(2):
            out_ref[g, odd] = sums[g][odd].astype(BF16)


def first_kernel(
    halo_ref, now_ref, back_ref, late_ref, gains_ref, table_ref, bank_ref, rest_ref, out_ref, left_ref
):
    pad = jnp.zeros((SPAN - PAST, FEEDS), BF16)
    sums = powers(
        early_bank(bank_ref),
        lambda c: jnp.concatenate(
            [pad, halo_ref[0, c], now_ref[0, c], pad, halo_ref[1, c], now_ref[1, c]], axis=0
        ),
        range(AHEAD), EARLY, gains_ref, table_ref, left_ref,
    )
    for g in range(EW):
        power = [
            late_ref[g, odd] + jnp.concatenate([sums[g][odd], back_ref[g, odd].astype(F32)], axis=0)
            for odd in range(2)
        ]
        out_ref[8 * g : 8 * (g + 1), :HALF] = by_beam(*power)


def join_kernel(got_ref, out_ref, joined_ref, sems):
    lane = lax.broadcasted_iota(jnp.int32, (1, 128), 1)
    low = lane < 64
    chunks = joined_ref.shape[0]
    pairs = GROUP // 2 // chunks
    copies = []
    for i in range(chunks):
        for p in range(pairs):
            s = pairs * i + p
            a = got_ref[2 * s].astype(F32)
            b = got_ref[2 * s + 1].astype(F32)
            first = jnp.where(low, a, pltpu.roll(b, 64, 1)).reshape(TIMES, HALF, 128)
            second = jnp.where(low, pltpu.roll(a, 64, 1), b).reshape(TIMES, HALF, 128)
            joined_ref[i, :, 0, :, 128 * p : 128 * (p + 1)] = jnp.swapaxes(first, 0, 1)
            joined_ref[i, :, 1, :, 128 * p : 128 * (p + 1)] = jnp.swapaxes(second, 0, 1)
        width = 128 * pairs
        copy = pltpu.make_async_copy(
            joined_ref.at[i], out_ref.at[:, :, :, pl.ds(width * i, width)], sems.at[i]
        )
        copy.start()
        copies.append(copy)
    for copy in copies:
        copy.wait()


def params(mib):
    return pltpu.CompilerParams(vmem_limit_bytes=mib << 20)


def cost(rows, moved):
    return pl.CostEstimate(flops=2 * rows * 512 * 512, bytes_accessed=moved, transcendentals=0)


VMEM = pl.BlockSpec(memory_space=pltpu.VMEM)
HBM = pl.BlockSpec(memory_space=pltpu.HBM)


def body(voltages, gains, window):
    count = lax.axis_size("tm")
    table = jnp.asarray(beam_table())

    window = window.reshape(1, FINE * TAPS)
    edge_scratch = [pltpu.VMEM((2, PAST, CHAN, FEEDS), BF16), pltpu.SemaphoreType.DMA((2,))]
    ahead, keep = pl.pallas_call(
        tail_kernel,
        in_specs=[HBM],
        out_specs=[VMEM] * 2,
        out_shape=[
            jax.ShapeDtypeStruct((2, AHEAD, PAST, FEEDS), BF16),
            jax.ShapeDtypeStruct((2, PAST, FEEDS), BF16),
        ],
        scratch_shapes=edge_scratch,
        compiler_params=params(51),
        name="block_tail",
    )(voltages)
    forward = [(i, (i + 1) % count) for i in range(count)]
    backward = [((i + 1) % count, i) for i in range(count)]
    halo = lax.ppermute(ahead, "tm", forward[:-1])
    back, first = pl.pallas_call(
        head_kernel,
        in_specs=[HBM],
        out_specs=[VMEM] * 2,
        out_shape=[
            jax.ShapeDtypeStruct((2, PAST, FEEDS), BF16),
            jax.ShapeDtypeStruct((2, CHAN, SPAN, FEEDS), BF16),
        ],
        scratch_shapes=[pltpu.VMEM((2, SPAN, CHAN, FEEDS), BF16), pltpu.SemaphoreType.DMA((2,))],
        compiler_params=params(46),
        name="block_head",
    )(voltages)
    head = lax.ppermute(back, "tm", backward)

    power_shape = jax.ShapeDtypeStruct((GROUP, TIMES * HALF, 128), BF16)
    rest, bank, late, second, blocks = pl.pallas_call(
        second_kernel,
        in_specs=[HBM] + [VMEM] * 4,
        out_specs=[VMEM] * 5,
        out_shape=[
            power_shape,
            jax.ShapeDtypeStruct((128, 256), BF16),
            jax.ShapeDtypeStruct((EW, 2, SPAN, NS // 2), F32),
            jax.ShapeDtypeStruct((2, CHAN, SPAN, FEEDS), BF16),
            jax.ShapeDtypeStruct((TIMES - 2, 2, SPAN, CHAN, FEEDS), BF16),
        ],
        scratch_shapes=[
            pltpu.VMEM((2, SPAN, CHAN, FEEDS), BF16),
            pltpu.VMEM((1024, 512), BF16),
            pltpu.SemaphoreType.DMA((TIMES - 1,)),
        ],
        compiler_params=params(42),
        cost_estimate=cost(1280, 4 << 20),
        name="second_time",
    )(voltages, first, gains, table, window)
    rest = pl.pallas_call(
        later_kernel,
        in_specs=[VMEM] * 6,
        out_specs=VMEM,
        out_shape=power_shape,
        scratch_shapes=[pltpu.VMEM((1024, 512), BF16)],
        input_output_aliases={5: 0},
        compiler_params=params(24),
        cost_estimate=cost(2048, 4 << 20),
        name="later_times",
    )(blocks, second, gains, table, bank, rest)
    keep, rest = lax.optimization_barrier((keep, rest))
    returned = pl.pallas_call(
        neighbour_kernel,
        in_specs=[VMEM] * 5,
        out_specs=VMEM,
        out_shape=jax.ShapeDtypeStruct((EW, 2, FINE, NS // 2), BF16),
        scratch_shapes=[pltpu.VMEM((192, 512), BF16)],
        compiler_params=params(16),
        cost_estimate=cost(192, 1 << 20),
        name="next_block",
    )(head, keep, gains, table, bank)
    returned = lax.ppermute(returned, "tm", forward)
    power = pl.pallas_call(
        first_kernel,
        in_specs=[VMEM] * 8,
        out_specs=VMEM,
        out_shape=power_shape,
        scratch_shapes=[pltpu.VMEM((576, 512), BF16)],
        input_output_aliases={7: 0},
        compiler_params=params(24),
        cost_estimate=cost(576, 3 << 20),
        name="first_time",
    )(halo, first, returned, late, gains, table, bank, rest)
    got = lax.all_to_all(power, "freq", split_axis=0, concat_axis=0, tiled=True)
    chunks = 4
    wide = GROUP * CHAN * FINE
    joined = pl.pallas_call(
        join_kernel,
        in_specs=[VMEM],
        out_specs=HBM,
        out_shape=jax.ShapeDtypeStruct((HALF, 2, TIMES, wide), F32),
        scratch_shapes=[
            pltpu.VMEM((chunks, HALF, 2, TIMES, wide // chunks), F32),
            pltpu.SemaphoreType.DMA((chunks,)),
        ],
        compiler_params=params(16),
        name="join_channels",
    )(got)
    return joined.reshape(GROUP, TIMES, wide)


def solution(mesh):
    placed = (P(None, "tm", "freq", None), P(None, "freq", None), P())
    return jax.shard_map(
        body, mesh=mesh, in_specs=placed, out_specs=P("freq", "tm", None), check_vma=False
    )
```

```python
import math

import jax
import jax.numpy as jnp
import numpy as np
from jax import lax
from jax.experimental import pallas as pl
from jax.experimental.pallas import tpu as pltpu
from jax.sharding import PartitionSpec as P

EW = 4
NS = 256
FEEDS = EW * NS
FINE = 16
TAPS = 4
INTEG = 4
CHAN = 4
AHEAD = 3
SPAN = INTEG * FINE
PAST = (TAPS - 1) * FINE
GROUP = 32
HALF = 16
TIMES = 4
EARLY = TAPS - 1

F32 = jnp.float32
BF16 = jnp.bfloat16


def beam_table():
    q = np.arange(NS // 2)[:, None]
    tables = []
    scale = 1.0 / math.sqrt(NS) / math.sqrt(EW) / math.sqrt(INTEG)
    for odd in range(2):
        k = 2 * np.arange(NS // 2)[None, :] + odd
        angle = (q * k % NS).astype(np.float32) * np.float32(2.0 * math.pi / NS)
        cos = np.cos(angle).astype(jnp.bfloat16).astype(np.float32)
        sin = np.sin(angle).astype(jnp.bfloat16).astype(np.float32)
        tables.append(np.block([[cos, -sin], [sin, cos]]) * np.float32(scale))
    return np.stack(tables).astype(jnp.bfloat16)


def fill_bank(window_ref, bank_ref):
    taps = jnp.concatenate([window_ref[...], jnp.zeros((1, 64), F32)], axis=1)
    lane = lax.broadcasted_iota(jnp.int32, (1, 2 * SPAN), 1)
    line = jnp.zeros((1, 2 * SPAN), F32)
    for m in range(TAPS):
        moved = pltpu.roll(taps, (64 - 32 * m) % 128, 1)
        line = jnp.where(lane // FINE == TAPS - m, moved, line)
    f = lax.broadcasted_iota(jnp.int32, (FINE, 2 * SPAN), 0)
    n = lax.broadcasted_iota(jnp.int32, (FINE, 2 * SPAN), 1) % FINE
    turn = f * n % FINE
    scale = 1.0 / math.sqrt(FINE * TAPS)
    cos = jnp.zeros((FINE, 2 * SPAN), F32)
    sin = jnp.zeros((FINE, 2 * SPAN), F32)
    for k in range(FINE):
        angle = 2.0 * math.pi * k / FINE
        cos = jnp.where(turn == k, scale * math.cos(angle), cos)
        sin = jnp.where(turn == k, scale * math.sin(angle), sin)
    for j in range(INTEG):
        row = line if j == 0 else pltpu.roll(line, FINE * j, 1)
        re, im = (cos * row).astype(BF16), (sin * row).astype(BF16)
        bank_ref[FINE * j : FINE * (j + 1), :128] = re
        bank_ref[FINE * j : FINE * (j + 1), 128:] = im
        bank_ref[64 + FINE * j : 64 + FINE * (j + 1), :128] = -im
        bank_ref[64 + FINE * j : 64 + FINE * (j + 1), 128:] = re


def steer(spec, gr, gi):
    half = spec.shape[0] // 2
    sr, si = spec[:half], spec[half:]
    cr = gr * sr - gi * si
    ci = gr * si + gi * sr
    r0, r1, r2, r3 = (cr[:, NS * e : NS * (e + 1)] for e in range(EW))
    i0, i1, i2, i3 = (ci[:, NS * e : NS * (e + 1)] for e in range(EW))
    rs, rd, it, iu = r0 + r2, r0 - r2, i0 + i2, i0 - i2
    rv, rw, iv, iw = r1 + r3, r1 - r3, i1 + i3, i1 - i3
    return (rs + rv, it + iv), (rd + iw, iu - rw), (rs - rv, it - iv), (rd - iw, iu + rw)


def powers(bank, data_of, channels, frames, gains_ref, table_ref, left_ref):
    count = len(channels)
    rows = frames * count * FINE
    for at, c in enumerate(channels):
        spec = jnp.dot(bank, data_of(c), preferred_element_type=F32)
        beams = steer(spec, gains_ref[0, c : c + 1], gains_ref[1, c : c + 1])
        for g in range(EW):
            for part in range(2):
                low, high = beams[g][part][:, :128], beams[g][part][:, 128:]
                for odd, value in enumerate((low + high, low - high)):
                    value = value.astype(BF16)
                    lane = 256 * odd + 128 * part
                    for j in range(frames):
                        row = rows * g + FINE * (count * j + at)
                        left_ref[row : row + FINE, lane : lane + 128] = value[FINE * j : FINE * (j + 1)]
    part = rows // frames
    step = EW if rows < 256 else 1
    sums = [[None, None] for _ in range(EW)]
    for g in range(0, EW, step):
        for odd in range(2):
            beam = jnp.dot(
                left_ref[rows * g : rows * (g + step), 256 * odd : 256 * (odd + 1)],
                table_ref[odd], preferred_element_type=F32,
            )
            re, im = beam[:, :128], beam[:, 128:]
            power = re * re + im * im
            for i in range(step):
                total = power[rows * i : rows * i + part]
                for j in range(1, frames):
                    total = total + power[rows * i + part * j : rows * i + part * (j + 1)]
                sums[g + i][odd] = total
    return sums


def by_beam(even, odd):
    power = jnp.concatenate([even, odd], axis=0)
    return power.T.astype(BF16).reshape(8, HALF, 128)


def early_bank(bank_ref):
    return jnp.concatenate([bank_ref[: FINE * EARLY], bank_ref[64 : 64 + FINE * EARLY]], axis=0)


def tail_kernel(volt_ref, ahead_ref, tail_ref, sems):
    start = volt_ref.shape[1] - PAST
    copies = [
        pltpu.make_async_copy(volt_ref.at[part, pl.ds(start, PAST)], tail_ref.at[part], sems.at[part])
        for part in range(2)
    ]
    for copy in copies:
        copy.start()
    for part in range(2):
        copies[part].wait()
        ahead_ref[part] = jnp.swapaxes(tail_ref[part], 0, 1)[:AHEAD]


def head_kernel(volt_ref, back_ref, first_ref, head_ref, sems):
    copies = [
        pltpu.make_async_copy(volt_ref.at[part, pl.ds(0, SPAN)], head_ref.at[part], sems.at[part])
        for part in range(2)
    ]
    for copy in copies:
        copy.start()
    for part in range(2):
        copies[part].wait()
        head = jnp.swapaxes(head_ref[part], 0, 1)
        first_ref[part] = head
        back_ref[part] = head[AHEAD, :PAST]


def form_time(at, past, now_ref, gains_ref, table_ref, bank_ref, out_ref, left_ref):
    now = [jnp.swapaxes(now_ref[part], 0, 1) for part in range(2)]
    sums = powers(
        bank_ref[...],
        lambda c: jnp.concatenate([past[0][c], now[0][c], past[1][c], now[1][c]], axis=0),
        range(CHAN), INTEG, gains_ref, table_ref, left_ref,
    )
    for g in range(EW):
        out_ref[8 * g : 8 * (g + 1), HALF * at : HALF * (at + 1)] = by_beam(*sums[g])
    return now


def second_kernel(
    volt_ref, first_ref, gains_ref, table_ref, window_ref,
    out_ref, bank_ref, late_ref, second_ref, ahead_ref, block_ref, left_ref, sems,
):
    to = [block_ref] + [ahead_ref.at[i] for i in range(TIMES - 2)]
    copies = [
        pltpu.make_async_copy(volt_ref.at[:, pl.ds(SPAN * (i + 1), SPAN)], to[i], sems.at[i])
        for i in range(TIMES - 1)
    ]
    for copy in copies:
        copy.start()
    fill_bank(window_ref, bank_ref)
    sums = powers(
        jnp.concatenate([bank_ref[48:64], bank_ref[112:128]], axis=0),
        lambda c: jnp.concatenate([first_ref[0, c], first_ref[0, c], first_ref[1, c], first_ref[1, c]], axis=0),
        range(CHAN), 1, gains_ref, table_ref, left_ref,
    )
    for g in range(EW):
        for odd in range(2):
            late_ref[g, odd] = sums[g][odd]
    copies[0].wait()
    now = form_time(0, first_ref, block_ref, gains_ref, table_ref, bank_ref, out_ref, left_ref)
    for part in range(2):
        second_ref[part] = now[part]
    for copy in copies[1:]:
        copy.wait()


def later_kernel(ahead_ref, second_ref, gains_ref, table_ref, bank_ref, out_ref, keep_ref, left_ref):
    now = form_time(0, second_ref, ahead_ref.at[0], gains_ref, table_ref, bank_ref, out_ref, left_ref)
    now = form_time(1, now, ahead_ref.at[1], gains_ref, table_ref, bank_ref, out_ref, left_ref)
    for part in range(2):
        keep_ref[part] = now[part][AHEAD, SPAN - PAST :]


def neighbour_kernel(head_ref, keep_ref, gains_ref, table_ref, bank_ref, out_ref, left_ref):
    last = lax.axis_index("tm") == lax.axis_size("tm") - 1
    bank = early_bank(bank_ref)
    lane = lax.broadcasted_iota(jnp.int32, bank.shape, 1)
    edge = jnp.where(last, SPAN, 0)
    bank = jnp.where(lane % 128 < edge, 0.0, bank.astype(F32)).astype(BF16)
    pad = jnp.zeros((SPAN - PAST, FEEDS), BF16)
    sums = powers(
        bank,
        lambda c: jnp.concatenate(
            [pad, keep_ref[0], head_ref[0], pad, pad, keep_ref[1], head_ref[1], pad], axis=0
        ),
        (AHEAD,), EARLY, gains_ref, table_ref, left_ref,
    )
    for g in range(EW):
        for odd in range(2):
            out_ref[g, odd] = sums[g][odd].astype(BF16)


def first_kernel(
    halo_ref, now_ref, back_ref, late_ref, gains_ref, table_ref, bank_ref, second_ref, later_ref,
    out_ref, left_ref,
):
    out_ref[:, HALF : 2 * HALF] = second_ref[...]
    out_ref[:, 2 * HALF :] = later_ref[...]
    pad = jnp.zeros((SPAN - PAST, FEEDS), BF16)
    sums = powers(
        early_bank(bank_ref),
        lambda c: jnp.concatenate(
            [pad, halo_ref[0, c], now_ref[0, c], pad, halo_ref[1, c], now_ref[1, c]], axis=0
        ),
        range(AHEAD), EARLY, gains_ref, table_ref, left_ref,
    )
    for g in range(EW):
        power = [
            late_ref[g, odd] + jnp.concatenate([sums[g][odd], back_ref[g, odd].astype(F32)], axis=0)
            for odd in range(2)
        ]
        out_ref[8 * g : 8 * (g + 1), :HALF] = by_beam(*power)


def join_kernel(got_ref, out_ref, joined_ref, sems):
    lane = lax.broadcasted_iota(jnp.int32, (1, 128), 1)
    low = lane < 64
    chunks = joined_ref.shape[0]
    pairs = GROUP // 2 // chunks
    copies = []
    for i in range(chunks):
        for p in range(pairs):
            s = pairs * i + p
            a = got_ref[2 * s].astype(F32)
            b = got_ref[2 * s + 1].astype(F32)
            first = jnp.where(low, a, pltpu.roll(b, 64, 1)).reshape(TIMES, HALF, 128)
            second = jnp.where(low, pltpu.roll(a, 64, 1), b).reshape(TIMES, HALF, 128)
            joined_ref[i, :, 0, :, 128 * p : 128 * (p + 1)] = jnp.swapaxes(first, 0, 1)
            joined_ref[i, :, 1, :, 128 * p : 128 * (p + 1)] = jnp.swapaxes(second, 0, 1)
        width = 128 * pairs
        copy = pltpu.make_async_copy(
            joined_ref.at[i], out_ref.at[:, :, :, pl.ds(width * i, width)], sems.at[i]
        )
        copy.start()
        copies.append(copy)
    for copy in copies:
        copy.wait()


def params(mib):
    return pltpu.CompilerParams(vmem_limit_bytes=mib << 20)


def cost(rows, moved):
    return pl.CostEstimate(flops=2 * rows * 512 * 512, bytes_accessed=moved, transcendentals=0)


VMEM = pl.BlockSpec(memory_space=pltpu.VMEM)
HBM = pl.BlockSpec(memory_space=pltpu.HBM)


def body(voltages, gains, window):
    count = lax.axis_size("tm")
    table = jnp.asarray(beam_table())

    window = window.reshape(1, FINE * TAPS)
    ahead = pl.pallas_call(
        tail_kernel,
        in_specs=[HBM],
        out_specs=VMEM,
        out_shape=jax.ShapeDtypeStruct((2, AHEAD, PAST, FEEDS), BF16),
        scratch_shapes=[pltpu.VMEM((2, PAST, CHAN, FEEDS), BF16), pltpu.SemaphoreType.DMA((2,))],
        compiler_params=params(51),
        name="block_tail",
    )(voltages)
    forward = [(i, (i + 1) % count) for i in range(count)]
    backward = [((i + 1) % count, i) for i in range(count)]
    halo = lax.ppermute(ahead, "tm", forward[:-1])
    back, first = pl.pallas_call(
        head_kernel,
        in_specs=[HBM],
        out_specs=[VMEM] * 2,
        out_shape=[
            jax.ShapeDtypeStruct((2, PAST, FEEDS), BF16),
            jax.ShapeDtypeStruct((2, CHAN, SPAN, FEEDS), BF16),
        ],
        scratch_shapes=[pltpu.VMEM((2, SPAN, CHAN, FEEDS), BF16), pltpu.SemaphoreType.DMA((2,))],
        compiler_params=params(46),
        name="block_head",
    )(voltages)
    head = lax.ppermute(back, "tm", backward)

    def powers_of(times):
        return jax.ShapeDtypeStruct((GROUP, times * HALF, 128), BF16)

    power_1, bank, late, second, blocks = pl.pallas_call(
        second_kernel,
        in_specs=[HBM] + [VMEM] * 4,
        out_specs=[VMEM] * 5,
        out_shape=[
            powers_of(1),
            jax.ShapeDtypeStruct((128, 256), BF16),
            jax.ShapeDtypeStruct((EW, 2, SPAN, NS // 2), F32),
            jax.ShapeDtypeStruct((2, CHAN, SPAN, FEEDS), BF16),
            jax.ShapeDtypeStruct((TIMES - 2, 2, SPAN, CHAN, FEEDS), BF16),
        ],
        scratch_shapes=[
            pltpu.VMEM((2, SPAN, CHAN, FEEDS), BF16),
            pltpu.VMEM((1024, 512), BF16),
            pltpu.SemaphoreType.DMA((TIMES - 1,)),
        ],
        compiler_params=params(42),
        cost_estimate=cost(1280, 4 << 20),
        name="second_time",
    )(voltages, first, gains, table, window)
    power_23, keep = pl.pallas_call(
        later_kernel,
        in_specs=[VMEM] * 5,
        out_specs=[VMEM] * 2,
        out_shape=[powers_of(TIMES - 2), jax.ShapeDtypeStruct((2, PAST, FEEDS), BF16)],
        scratch_shapes=[pltpu.VMEM((1024, 512), BF16)],
        compiler_params=params(24),
        cost_estimate=cost(2048, 4 << 20),
        name="later_times",
    )(blocks, second, gains, table, bank)
    returned = pl.pallas_call(
        neighbour_kernel,
        in_specs=[VMEM] * 5,
        out_specs=VMEM,
        out_shape=jax.ShapeDtypeStruct((EW, 2, FINE, NS // 2), BF16),
        scratch_shapes=[pltpu.VMEM((192, 512), BF16)],
        compiler_params=params(16),
        cost_estimate=cost(192, 1 << 20),
        name="next_block",
    )(head, keep, gains, table, bank)
    returned = lax.ppermute(returned, "tm", forward)
    power = pl.pallas_call(
        first_kernel,
        in_specs=[VMEM] * 9,
        out_specs=VMEM,
        out_shape=powers_of(TIMES),
        scratch_shapes=[pltpu.VMEM((576, 512), BF16)],
        compiler_params=params(24),
        cost_estimate=cost(576, 3 << 20),
        name="first_time",
    )(halo, first, returned, late, gains, table, bank, power_1, power_23)
    got = lax.all_to_all(power, "freq", split_axis=0, concat_axis=0, tiled=True)
    chunks = 8
    wide = GROUP * CHAN * FINE
    joined = pl.pallas_call(
        join_kernel,
        in_specs=[VMEM],
        out_specs=HBM,
        out_shape=jax.ShapeDtypeStruct((HALF, 2, TIMES, wide), F32),
        scratch_shapes=[
            pltpu.VMEM((chunks, HALF, 2, TIMES, wide // chunks), F32),
            pltpu.SemaphoreType.DMA((chunks,)),
        ],
        compiler_params=params(16),
        name="join_channels",
    )(got)
    return joined.reshape(GROUP, TIMES, wide)


def solution(mesh):
    placed = (P(None, "tm", "freq", None), P(None, "freq", None), P())
    return jax.shard_map(
        body, mesh=mesh, in_specs=placed, out_specs=P("freq", "tm", None), check_vma=False
    )
```

```python
import math

import jax
import jax.numpy as jnp
import numpy as np
from jax import lax
from jax.experimental import pallas as pl
from jax.experimental.pallas import tpu as pltpu
from jax.sharding import PartitionSpec as P

EW = 4
NS = 256
FEEDS = EW * NS
FINE = 16
TAPS = 4
INTEG = 4
CHAN = 4
AHEAD = 3
SPAN = INTEG * FINE
PAST = (TAPS - 1) * FINE
GROUP = 32
HALF = 16
TIMES = 4
EARLY = TAPS - 1

F32 = jnp.float32
BF16 = jnp.bfloat16


def beam_table():
    q = np.arange(NS // 2)[:, None]
    tables = []
    scale = 1.0 / math.sqrt(NS) / math.sqrt(EW) / math.sqrt(INTEG)
    for odd in range(2):
        k = 2 * np.arange(NS // 2)[None, :] + odd
        angle = (q * k % NS).astype(np.float32) * np.float32(2.0 * math.pi / NS)
        cos = np.cos(angle).astype(jnp.bfloat16).astype(np.float32)
        sin = np.sin(angle).astype(jnp.bfloat16).astype(np.float32)
        tables.append(np.block([[cos, -sin], [sin, cos]]) * np.float32(scale))
    return np.stack(tables).astype(jnp.bfloat16)


def fill_bank(window_ref, bank_ref):
    taps = jnp.concatenate([window_ref[...], jnp.zeros((1, 64), F32)], axis=1)
    lane = lax.broadcasted_iota(jnp.int32, (1, 2 * SPAN), 1)
    line = jnp.zeros((1, 2 * SPAN), F32)
    for m in range(TAPS):
        moved = pltpu.roll(taps, (64 - 32 * m) % 128, 1)
        line = jnp.where(lane // FINE == TAPS - m, moved, line)
    f = lax.broadcasted_iota(jnp.int32, (FINE, 2 * SPAN), 0)
    n = lax.broadcasted_iota(jnp.int32, (FINE, 2 * SPAN), 1) % FINE
    turn = f * n % FINE
    scale = 1.0 / math.sqrt(FINE * TAPS)
    cos = jnp.zeros((FINE, 2 * SPAN), F32)
    sin = jnp.zeros((FINE, 2 * SPAN), F32)
    for k in range(FINE):
        angle = 2.0 * math.pi * k / FINE
        cos = jnp.where(turn == k, scale * math.cos(angle), cos)
        sin = jnp.where(turn == k, scale * math.sin(angle), sin)
    for j in range(INTEG):
        row = line if j == 0 else pltpu.roll(line, FINE * j, 1)
        re, im = (cos * row).astype(BF16), (sin * row).astype(BF16)
        bank_ref[FINE * j : FINE * (j + 1), :128] = re
        bank_ref[FINE * j : FINE * (j + 1), 128:] = im
        bank_ref[64 + FINE * j : 64 + FINE * (j + 1), :128] = -im
        bank_ref[64 + FINE * j : 64 + FINE * (j + 1), 128:] = re


def steer(spec, gr, gi):
    half = spec.shape[0] // 2
    sr, si = spec[:half], spec[half:]
    cr = gr * sr - gi * si
    ci = gr * si + gi * sr
    r0, r1, r2, r3 = (cr[:, NS * e : NS * (e + 1)] for e in range(EW))
    i0, i1, i2, i3 = (ci[:, NS * e : NS * (e + 1)] for e in range(EW))
    rs, rd, it, iu = r0 + r2, r0 - r2, i0 + i2, i0 - i2
    rv, rw, iv, iw = r1 + r3, r1 - r3, i1 + i3, i1 - i3
    return (rs + rv, it + iv), (rd + iw, iu - rw), (rs - rv, it - iv), (rd - iw, iu + rw)


def powers(bank, data_of, channels, frames, gains_ref, table_ref, left_ref, known_ref=None):
    count = len(channels)
    rows = frames * count * FINE
    for at, c in enumerate(channels):
        spec = jnp.dot(bank, data_of(c), preferred_element_type=F32)
        if known_ref is not None:
            spec = spec + known_ref[c]
        beams = steer(spec, gains_ref[0, c : c + 1], gains_ref[1, c : c + 1])
        for g in range(EW):
            for part in range(2):
                low, high = beams[g][part][:, :128], beams[g][part][:, 128:]
                for odd, value in enumerate((low + high, low - high)):
                    value = value.astype(BF16)
                    lane = 256 * odd + 128 * part
                    for j in range(frames):
                        row = rows * g + FINE * (count * j + at)
                        left_ref[row : row + FINE, lane : lane + 128] = value[FINE * j : FINE * (j + 1)]
    part = rows // frames
    step = EW if rows < 256 else 1
    sums = [[None, None] for _ in range(EW)]
    for g in range(0, EW, step):
        for odd in range(2):
            beam = jnp.dot(
                left_ref[rows * g : rows * (g + step), 256 * odd : 256 * (odd + 1)],
                table_ref[odd], preferred_element_type=F32,
            )
            re, im = beam[:, :128], beam[:, 128:]
            power = re * re + im * im
            for i in range(step):
                total = power[rows * i : rows * i + part]
                for j in range(1, frames):
                    total = total + power[rows * i + part * j : rows * i + part * (j + 1)]
                sums[g + i][odd] = total
    return sums


def by_beam(even, odd):
    power = jnp.concatenate([even, odd], axis=0)
    return power.T.astype(BF16).reshape(8, HALF, 128)


def early_bank(bank_ref):
    return jnp.concatenate([bank_ref[: FINE * EARLY], bank_ref[64 : 64 + FINE * EARLY]], axis=0)


def half_bank(bank_ref, now):
    bank, at = early_bank(bank_ref), SPAN * now
    return jnp.concatenate([bank[:, at : at + SPAN], bank[:, 128 + at : 128 + at + SPAN]], axis=1)


def tail_kernel(volt_ref, ahead_ref, tail_ref, sems):
    start = volt_ref.shape[1] - PAST
    copies = [
        pltpu.make_async_copy(volt_ref.at[part, pl.ds(start, PAST)], tail_ref.at[part], sems.at[part])
        for part in range(2)
    ]
    for copy in copies:
        copy.start()
    for part in range(2):
        copies[part].wait()
        ahead_ref[part] = jnp.swapaxes(tail_ref[part], 0, 1)[:AHEAD]


def head_kernel(volt_ref, back_ref, first_ref, head_ref, sems):
    copies = [
        pltpu.make_async_copy(volt_ref.at[part, pl.ds(0, SPAN)], head_ref.at[part], sems.at[part])
        for part in range(2)
    ]
    for copy in copies:
        copy.start()
    for part in range(2):
        copies[part].wait()
        head = jnp.swapaxes(head_ref[part], 0, 1)
        first_ref[part] = head
        back_ref[part] = head[AHEAD, :PAST]


def form_time(at, past, now_ref, gains_ref, table_ref, bank_ref, out_ref, left_ref):
    now = [jnp.swapaxes(now_ref[part], 0, 1) for part in range(2)]
    sums = powers(
        bank_ref[...],
        lambda c: jnp.concatenate([past[0][c], now[0][c], past[1][c], now[1][c]], axis=0),
        range(CHAN), INTEG, gains_ref, table_ref, left_ref,
    )
    for g in range(EW):
        out_ref[8 * g : 8 * (g + 1), HALF * at : HALF * (at + 1)] = by_beam(*sums[g])
    return now


def second_kernel(
    volt_ref, first_ref, gains_ref, table_ref, window_ref,
    out_ref, bank_ref, known_ref, late_ref, second_ref, ahead_ref, block_ref, left_ref, sems,
):
    to = [block_ref] + [ahead_ref.at[i] for i in range(TIMES - 2)]
    copies = [
        pltpu.make_async_copy(volt_ref.at[:, pl.ds(SPAN * (i + 1), SPAN)], to[i], sems.at[i])
        for i in range(TIMES - 1)
    ]
    for copy in copies:
        copy.start()
    fill_bank(window_ref, bank_ref)
    for c in range(AHEAD):
        own = jnp.concatenate([first_ref[0, c], first_ref[1, c]], axis=0)
        known_ref[c] = jnp.dot(half_bank(bank_ref, 1), own, preferred_element_type=F32)
    sums = powers(
        jnp.concatenate([bank_ref[48:64], bank_ref[112:128]], axis=0),
        lambda c: jnp.concatenate([first_ref[0, c], first_ref[0, c], first_ref[1, c], first_ref[1, c]], axis=0),
        range(CHAN), 1, gains_ref, table_ref, left_ref,
    )
    for g in range(EW):
        for odd in range(2):
            late_ref[g, odd] = sums[g][odd]
    copies[0].wait()
    now = form_time(0, first_ref, block_ref, gains_ref, table_ref, bank_ref, out_ref, left_ref)
    for part in range(2):
        second_ref[part] = now[part]
    for copy in copies[1:]:
        copy.wait()


def later_kernel(ahead_ref, second_ref, gains_ref, table_ref, bank_ref, out_ref, keep_ref, left_ref):
    now = form_time(0, second_ref, ahead_ref.at[0], gains_ref, table_ref, bank_ref, out_ref, left_ref)
    now = form_time(1, now, ahead_ref.at[1], gains_ref, table_ref, bank_ref, out_ref, left_ref)
    for part in range(2):
        keep_ref[part] = now[part][AHEAD, SPAN - PAST :]


def neighbour_kernel(head_ref, keep_ref, gains_ref, table_ref, bank_ref, out_ref, left_ref):
    last = lax.axis_index("tm") == lax.axis_size("tm") - 1
    bank = early_bank(bank_ref)
    lane = lax.broadcasted_iota(jnp.int32, bank.shape, 1)
    edge = jnp.where(last, SPAN, 0)
    bank = jnp.where(lane % 128 < edge, 0.0, bank.astype(F32)).astype(BF16)
    pad = jnp.zeros((SPAN - PAST, FEEDS), BF16)
    sums = powers(
        bank,
        lambda c: jnp.concatenate(
            [pad, keep_ref[0], head_ref[0], pad, pad, keep_ref[1], head_ref[1], pad], axis=0
        ),
        (AHEAD,), EARLY, gains_ref, table_ref, left_ref,
    )
    for g in range(EW):
        for odd in range(2):
            out_ref[g, odd] = sums[g][odd].astype(BF16)


def first_kernel(
    halo_ref, known_ref, back_ref, late_ref, gains_ref, table_ref, bank_ref, second_ref, later_ref,
    out_ref, left_ref,
):
    out_ref[:, HALF : 2 * HALF] = second_ref[...]
    out_ref[:, 2 * HALF :] = later_ref[...]
    pad = jnp.zeros((SPAN - PAST, FEEDS), BF16)
    sums = powers(
        half_bank(bank_ref, 0),
        lambda c: jnp.concatenate(
            [pad, halo_ref[0, c], pad, halo_ref[1, c]], axis=0
        ),
        range(AHEAD), EARLY, gains_ref, table_ref, left_ref, known_ref,
    )
    for g in range(EW):
        power = [
            late_ref[g, odd] + jnp.concatenate([sums[g][odd], back_ref[g, odd].astype(F32)], axis=0)
            for odd in range(2)
        ]
        out_ref[8 * g : 8 * (g + 1), :HALF] = by_beam(*power)


def join_kernel(got_ref, out_ref, joined_ref, sems):
    lane = lax.broadcasted_iota(jnp.int32, (1, 128), 1)
    low = lane < 64
    chunks = joined_ref.shape[0]
    pairs = GROUP // 2 // chunks
    copies = []
    for i in range(chunks):
        for p in range(pairs):
            s = pairs * i + p
            a = got_ref[2 * s].astype(F32)
            b = got_ref[2 * s + 1].astype(F32)
            first = jnp.where(low, a, pltpu.roll(b, 64, 1)).reshape(TIMES, HALF, 128)
            second = jnp.where(low, pltpu.roll(a, 64, 1), b).reshape(TIMES, HALF, 128)
            joined_ref[i, :, 0, :, 128 * p : 128 * (p + 1)] = jnp.swapaxes(first, 0, 1)
            joined_ref[i, :, 1, :, 128 * p : 128 * (p + 1)] = jnp.swapaxes(second, 0, 1)
        width = 128 * pairs
        copy = pltpu.make_async_copy(
            joined_ref.at[i], out_ref.at[:, :, :, pl.ds(width * i, width)], sems.at[i]
        )
        copy.start()
        copies.append(copy)
    for copy in copies:
        copy.wait()


def params(mib):
    return pltpu.CompilerParams(vmem_limit_bytes=mib << 20)


def cost(rows, moved):
    return pl.CostEstimate(flops=2 * rows * 512 * 512, bytes_accessed=moved, transcendentals=0)


VMEM = pl.BlockSpec(memory_space=pltpu.VMEM)
HBM = pl.BlockSpec(memory_space=pltpu.HBM)


def body(voltages, gains, window):
    count = lax.axis_size("tm")
    table = jnp.asarray(beam_table())

    window = window.reshape(1, FINE * TAPS)
    ahead = pl.pallas_call(
        tail_kernel,
        in_specs=[HBM],
        out_specs=VMEM,
        out_shape=jax.ShapeDtypeStruct((2, AHEAD, PAST, FEEDS), BF16),
        scratch_shapes=[pltpu.VMEM((2, PAST, CHAN, FEEDS), BF16), pltpu.SemaphoreType.DMA((2,))],
        compiler_params=params(51),
        name="block_tail",
    )(voltages)
    forward = [(i, (i + 1) % count) for i in range(count)]
    backward = [((i + 1) % count, i) for i in range(count)]
    halo = lax.ppermute(ahead, "tm", forward[:-1])
    back, first = pl.pallas_call(
        head_kernel,
        in_specs=[HBM],
        out_specs=[VMEM] * 2,
        out_shape=[
            jax.ShapeDtypeStruct((2, PAST, FEEDS), BF16),
            jax.ShapeDtypeStruct((2, CHAN, SPAN, FEEDS), BF16),
        ],
        scratch_shapes=[pltpu.VMEM((2, SPAN, CHAN, FEEDS), BF16), pltpu.SemaphoreType.DMA((2,))],
        compiler_params=params(46),
        name="block_head",
    )(voltages)
    head = lax.ppermute(back, "tm", backward)

    def powers_of(times):
        return jax.ShapeDtypeStruct((GROUP, times * HALF, 128), BF16)

    power_1, bank, known, late, second, blocks = pl.pallas_call(
        second_kernel,
        in_specs=[HBM] + [VMEM] * 4,
        out_specs=[VMEM] * 6,
        out_shape=[
            powers_of(1),
            jax.ShapeDtypeStruct((128, 256), BF16),
            jax.ShapeDtypeStruct((AHEAD, 2 * EARLY * FINE, FEEDS), F32),
            jax.ShapeDtypeStruct((EW, 2, SPAN, NS // 2), F32),
            jax.ShapeDtypeStruct((2, CHAN, SPAN, FEEDS), BF16),
            jax.ShapeDtypeStruct((TIMES - 2, 2, SPAN, CHAN, FEEDS), BF16),
        ],
        scratch_shapes=[
            pltpu.VMEM((2, SPAN, CHAN, FEEDS), BF16),
            pltpu.VMEM((1024, 512), BF16),
            pltpu.SemaphoreType.DMA((TIMES - 1,)),
        ],
        compiler_params=params(42),
        cost_estimate=cost(1280, 4 << 20),
        name="second_time",
    )(voltages, first, gains, table, window)
    power_23, keep = pl.pallas_call(
        later_kernel,
        in_specs=[VMEM] * 5,
        out_specs=[VMEM] * 2,
        out_shape=[powers_of(TIMES - 2), jax.ShapeDtypeStruct((2, PAST, FEEDS), BF16)],
        scratch_shapes=[pltpu.VMEM((1024, 512), BF16)],
        compiler_params=params(24),
        cost_estimate=cost(2048, 4 << 20),
        name="later_times",
    )(blocks, second, gains, table, bank)
    returned = pl.pallas_call(
        neighbour_kernel,
        in_specs=[VMEM] * 5,
        out_specs=VMEM,
        out_shape=jax.ShapeDtypeStruct((EW, 2, FINE, NS // 2), BF16),
        scratch_shapes=[pltpu.VMEM((192, 512), BF16)],
        compiler_params=params(16),
        cost_estimate=cost(192, 1 << 20),
        name="next_block",
    )(head, keep, gains, table, bank)
    returned = lax.ppermute(returned, "tm", forward)
    power = pl.pallas_call(
        first_kernel,
        in_specs=[VMEM] * 9,
        out_specs=VMEM,
        out_shape=powers_of(TIMES),
        scratch_shapes=[pltpu.VMEM((576, 512), BF16)],
        compiler_params=params(24),
        cost_estimate=cost(576, 3 << 20),
        name="first_time",
    )(halo, known, returned, late, gains, table, bank, power_1, power_23)
    got = lax.all_to_all(power, "freq", split_axis=0, concat_axis=0, tiled=True)
    chunks = 8
    wide = GROUP * CHAN * FINE
    joined = pl.pallas_call(
        join_kernel,
        in_specs=[VMEM],
        out_specs=HBM,
        out_shape=jax.ShapeDtypeStruct((HALF, 2, TIMES, wide), F32),
        scratch_shapes=[
            pltpu.VMEM((chunks, HALF, 2, TIMES, wide // chunks), F32),
            pltpu.SemaphoreType.DMA((chunks,)),
        ],
        compiler_params=params(16),
        name="join_channels",
    )(got)
    return joined.reshape(GROUP, TIMES, wide)


def solution(mesh):
    placed = (P(None, "tm", "freq", None), P(None, "freq", None), P())
    return jax.shard_map(
        body, mesh=mesh, in_specs=placed, out_specs=P("freq", "tm", None), check_vma=False
    )
```

```python
import math

import jax
import jax.numpy as jnp
import numpy as np
from jax import lax
from jax.experimental import pallas as pl
from jax.experimental.pallas import tpu as pltpu
from jax.sharding import PartitionSpec as P

EW = 4
NS = 256
FEEDS = EW * NS
FINE = 16
TAPS = 4
INTEG = 4
CHAN = 4
AHEAD = 3
SPAN = INTEG * FINE
PAST = (TAPS - 1) * FINE
GROUP = 32
HALF = 16
TIMES = 4
EARLY = TAPS - 1

F32 = jnp.float32
BF16 = jnp.bfloat16


def beam_table():
    q = np.arange(NS // 2)[:, None]
    tables = []
    scale = 1.0 / math.sqrt(NS) / math.sqrt(EW) / math.sqrt(INTEG)
    for odd in range(2):
        k = 2 * np.arange(NS // 2)[None, :] + odd
        angle = (q * k % NS).astype(np.float32) * np.float32(2.0 * math.pi / NS)
        cos = np.cos(angle).astype(jnp.bfloat16).astype(np.float32)
        sin = np.sin(angle).astype(jnp.bfloat16).astype(np.float32)
        tables.append(np.block([[cos, -sin], [sin, cos]]) * np.float32(scale))
    return np.stack(tables).astype(jnp.bfloat16)


def fill_bank(window_ref, bank_ref):
    taps = jnp.concatenate([window_ref[...], jnp.zeros((1, 64), F32)], axis=1)
    lane = lax.broadcasted_iota(jnp.int32, (1, 2 * SPAN), 1)
    line = jnp.zeros((1, 2 * SPAN), F32)
    for m in range(TAPS):
        moved = pltpu.roll(taps, (64 - 32 * m) % 128, 1)
        line = jnp.where(lane // FINE == TAPS - m, moved, line)
    f = lax.broadcasted_iota(jnp.int32, (FINE, 2 * SPAN), 0)
    n = lax.broadcasted_iota(jnp.int32, (FINE, 2 * SPAN), 1) % FINE
    turn = f * n % FINE
    scale = 1.0 / math.sqrt(FINE * TAPS)
    cos = jnp.zeros((FINE, 2 * SPAN), F32)
    sin = jnp.zeros((FINE, 2 * SPAN), F32)
    for k in range(FINE):
        angle = 2.0 * math.pi * k / FINE
        cos = jnp.where(turn == k, scale * math.cos(angle), cos)
        sin = jnp.where(turn == k, scale * math.sin(angle), sin)
    for j in range(INTEG):
        row = line if j == 0 else pltpu.roll(line, FINE * j, 1)
        re, im = (cos * row).astype(BF16), (sin * row).astype(BF16)
        bank_ref[FINE * j : FINE * (j + 1), :128] = re
        bank_ref[FINE * j : FINE * (j + 1), 128:] = im
        bank_ref[64 + FINE * j : 64 + FINE * (j + 1), :128] = -im
        bank_ref[64 + FINE * j : 64 + FINE * (j + 1), 128:] = re


def steer(spec, gr, gi):
    half = spec.shape[0] // 2
    sr, si = spec[:half], spec[half:]
    cr = gr * sr - gi * si
    ci = gr * si + gi * sr
    r0, r1, r2, r3 = (cr[:, NS * e : NS * (e + 1)] for e in range(EW))
    i0, i1, i2, i3 = (ci[:, NS * e : NS * (e + 1)] for e in range(EW))
    rs, rd, it, iu = r0 + r2, r0 - r2, i0 + i2, i0 - i2
    rv, rw, iv, iw = r1 + r3, r1 - r3, i1 + i3, i1 - i3
    return (rs + rv, it + iv), (rd + iw, iu - rw), (rs - rv, it - iv), (rd - iw, iu + rw)


def powers(bank, data_of, channels, frames, gains_ref, table_ref, left_ref):
    count = len(channels)
    rows = frames * count * FINE
    for at, c in enumerate(channels):
        spec = jnp.dot(bank, data_of(c), preferred_element_type=F32)
        beams = steer(spec, gains_ref[0, c : c + 1], gains_ref[1, c : c + 1])
        for g in range(EW):
            for part in range(2):
                low, high = beams[g][part][:, :128], beams[g][part][:, 128:]
                for odd, value in enumerate((low + high, low - high)):
                    value = value.astype(BF16)
                    lane = 256 * odd + 128 * part
                    for j in range(frames):
                        row = rows * g + FINE * (count * j + at)
                        left_ref[row : row + FINE, lane : lane + 128] = value[FINE * j : FINE * (j + 1)]
    part = rows // frames
    step = EW if rows < 256 else 1
    sums = [[None, None] for _ in range(EW)]
    for g in range(0, EW, step):
        for odd in range(2):
            beam = jnp.dot(
                left_ref[rows * g : rows * (g + step), 256 * odd : 256 * (odd + 1)],
                table_ref[odd], preferred_element_type=F32,
            )
            re, im = beam[:, :128], beam[:, 128:]
            power = re * re + im * im
            for i in range(step):
                total = power[rows * i : rows * i + part]
                for j in range(1, frames):
                    total = total + power[rows * i + part * j : rows * i + part * (j + 1)]
                sums[g + i][odd] = total
    return sums


def by_beam(even, odd):
    power = jnp.concatenate([even, odd], axis=0)
    return power.T.astype(BF16).reshape(8, HALF, 128)


def early_bank(bank_ref):
    return jnp.concatenate([bank_ref[: FINE * EARLY], bank_ref[64 : 64 + FINE * EARLY]], axis=0)


def tail_kernel(volt_ref, ahead_ref, tail_ref, sems):
    start = volt_ref.shape[1] - PAST
    copies = [
        pltpu.make_async_copy(volt_ref.at[part, pl.ds(start, PAST)], tail_ref.at[part], sems.at[part])
        for part in range(2)
    ]
    for copy in copies:
        copy.start()
    for part in range(2):
        copies[part].wait()
        ahead_ref[part] = jnp.swapaxes(tail_ref[part], 0, 1)[:AHEAD]


def head_kernel(volt_ref, back_ref, first_ref, head_ref, sems):
    copies = [
        pltpu.make_async_copy(volt_ref.at[part, pl.ds(0, SPAN)], head_ref.at[part], sems.at[part])
        for part in range(2)
    ]
    for copy in copies:
        copy.start()
    for part in range(2):
        copies[part].wait()
        head = jnp.swapaxes(head_ref[part], 0, 1)
        first_ref[part] = head
        back_ref[part] = head[AHEAD, :PAST]


def form_time(at, past, now_ref, gains_ref, table_ref, bank_ref, out_ref, left_ref):
    now = [jnp.swapaxes(now_ref[part], 0, 1) for part in range(2)]
    sums = powers(
        bank_ref[...],
        lambda c: jnp.concatenate([past[0][c], now[0][c], past[1][c], now[1][c]], axis=0),
        range(CHAN), INTEG, gains_ref, table_ref, left_ref,
    )
    for g in range(EW):
        out_ref[8 * g : 8 * (g + 1), HALF * at : HALF * (at + 1)] = by_beam(*sums[g])
    return now


def second_kernel(
    volt_ref, first_ref, gains_ref, table_ref, window_ref,
    out_ref, bank_ref, late_ref, second_ref, ahead_ref, block_ref, left_ref, sems,
):
    to = [block_ref] + [ahead_ref.at[i] for i in range(TIMES - 2)]
    copies = [
        pltpu.make_async_copy(volt_ref.at[:, pl.ds(SPAN * (i + 1), SPAN)], to[i], sems.at[i])
        for i in range(TIMES - 1)
    ]
    for copy in copies:
        copy.start()
    fill_bank(window_ref, bank_ref)
    sums = powers(
        jnp.concatenate([bank_ref[48:64], bank_ref[112:128]], axis=0),
        lambda c: jnp.concatenate([first_ref[0, c], first_ref[0, c], first_ref[1, c], first_ref[1, c]], axis=0),
        range(CHAN), 1, gains_ref, table_ref, left_ref,
    )
    for g in range(EW):
        for odd in range(2):
            late_ref[g, odd] = sums[g][odd]
    copies[0].wait()
    now = form_time(0, first_ref, block_ref, gains_ref, table_ref, bank_ref, out_ref, left_ref)
    for part in range(2):
        second_ref[part] = now[part]
    for copy in copies[1:]:
        copy.wait()


def later_kernel(ahead_ref, second_ref, gains_ref, table_ref, bank_ref, out_ref, keep_ref, left_ref):
    now = form_time(0, second_ref, ahead_ref.at[0], gains_ref, table_ref, bank_ref, out_ref, left_ref)
    now = form_time(1, now, ahead_ref.at[1], gains_ref, table_ref, bank_ref, out_ref, left_ref)
    for part in range(2):
        keep_ref[part] = now[part][AHEAD, SPAN - PAST :]


def neighbour_kernel(head_ref, keep_ref, gains_ref, table_ref, bank_ref, out_ref, left_ref):
    last = lax.axis_index("tm") == lax.axis_size("tm") - 1
    bank = early_bank(bank_ref)
    lane = lax.broadcasted_iota(jnp.int32, bank.shape, 1)
    edge = jnp.where(last, SPAN, 0)
    bank = jnp.where(lane % 128 < edge, 0.0, bank.astype(F32)).astype(BF16)
    pad = jnp.zeros((SPAN - PAST, FEEDS), BF16)
    sums = powers(
        bank,
        lambda c: jnp.concatenate(
            [pad, keep_ref[0], head_ref[0], pad, pad, keep_ref[1], head_ref[1], pad], axis=0
        ),
        (AHEAD,), EARLY, gains_ref, table_ref, left_ref,
    )
    for g in range(EW):
        for odd in range(2):
            out_ref[g, odd] = sums[g][odd].astype(BF16)


def first_kernel(
    halo_ref, now_ref, back_ref, late_ref, gains_ref, table_ref, bank_ref, second_ref, later_ref,
    out_ref, left_ref,
):
    pad = jnp.zeros((SPAN - PAST, FEEDS), BF16)
    sums = powers(
        early_bank(bank_ref),
        lambda c: jnp.concatenate(
            [pad, halo_ref[0, c], now_ref[0, c], pad, halo_ref[1, c], now_ref[1, c]], axis=0
        ),
        range(AHEAD), EARLY, gains_ref, table_ref, left_ref,
    )
    for g in range(EW):
        power = [
            late_ref[g, odd] + jnp.concatenate([sums[g][odd], back_ref[g, odd].astype(F32)], axis=0)
            for odd in range(2)
        ]
        out_ref[8 * g : 8 * (g + 1), :HALF] = by_beam(*power)
    out_ref[:, HALF : 2 * HALF] = second_ref[...]
    out_ref[:, 2 * HALF :] = later_ref[...]


def join_kernel(got_ref, out_ref, joined_ref, sems):
    lane = lax.broadcasted_iota(jnp.int32, (1, 128), 1)
    low = lane < 64
    chunks = joined_ref.shape[0]
    pairs = GROUP // 2 // chunks
    copies = []
    for i in range(chunks):
        for p in range(pairs):
            s = pairs * i + p
            a = got_ref[2 * s].astype(F32)
            b = got_ref[2 * s + 1].astype(F32)
            first = jnp.where(low, a, pltpu.roll(b, 64, 1)).reshape(TIMES, HALF, 128)
            second = jnp.where(low, pltpu.roll(a, 64, 1), b).reshape(TIMES, HALF, 128)
            joined_ref[i, :, 0, :, 128 * p : 128 * (p + 1)] = jnp.swapaxes(first, 0, 1)
            joined_ref[i, :, 1, :, 128 * p : 128 * (p + 1)] = jnp.swapaxes(second, 0, 1)
        width = 128 * pairs
        copy = pltpu.make_async_copy(
            joined_ref.at[i], out_ref.at[:, :, :, pl.ds(width * i, width)], sems.at[i]
        )
        copy.start()
        copies.append(copy)
    for copy in copies:
        copy.wait()


def params(mib):
    return pltpu.CompilerParams(vmem_limit_bytes=mib << 20)


def cost(rows, moved):
    return pl.CostEstimate(flops=2 * rows * 512 * 512, bytes_accessed=moved, transcendentals=0)


VMEM = pl.BlockSpec(memory_space=pltpu.VMEM)
HBM = pl.BlockSpec(memory_space=pltpu.HBM)


def body(voltages, gains, window):
    count = lax.axis_size("tm")
    table = jnp.asarray(beam_table())

    window = window.reshape(1, FINE * TAPS)
    ahead = pl.pallas_call(
        tail_kernel,
        in_specs=[HBM],
        out_specs=VMEM,
        out_shape=jax.ShapeDtypeStruct((2, AHEAD, PAST, FEEDS), BF16),
        scratch_shapes=[pltpu.VMEM((2, PAST, CHAN, FEEDS), BF16), pltpu.SemaphoreType.DMA((2,))],
        compiler_params=params(51),
        name="block_tail",
    )(voltages)
    forward = [(i, (i + 1) % count) for i in range(count)]
    backward = [((i + 1) % count, i) for i in range(count)]
    halo = lax.ppermute(ahead, "tm", forward[:-1])
    back, first = pl.pallas_call(
        head_kernel,
        in_specs=[HBM],
        out_specs=[VMEM] * 2,
        out_shape=[
            jax.ShapeDtypeStruct((2, PAST, FEEDS), BF16),
            jax.ShapeDtypeStruct((2, CHAN, SPAN, FEEDS), BF16),
        ],
        scratch_shapes=[pltpu.VMEM((2, SPAN, CHAN, FEEDS), BF16), pltpu.SemaphoreType.DMA((2,))],
        compiler_params=params(46),
        name="block_head",
    )(voltages)
    head = lax.ppermute(back, "tm", backward)

    def powers_of(times):
        return jax.ShapeDtypeStruct((GROUP, times * HALF, 128), BF16)

    power_1, bank, late, second, blocks = pl.pallas_call(
        second_kernel,
        in_specs=[HBM] + [VMEM] * 4,
        out_specs=[VMEM] * 5,
        out_shape=[
            powers_of(1),
            jax.ShapeDtypeStruct((128, 256), BF16),
            jax.ShapeDtypeStruct((EW, 2, SPAN, NS // 2), F32),
            jax.ShapeDtypeStruct((2, CHAN, SPAN, FEEDS), BF16),
            jax.ShapeDtypeStruct((TIMES - 2, 2, SPAN, CHAN, FEEDS), BF16),
        ],
        scratch_shapes=[
            pltpu.VMEM((2, SPAN, CHAN, FEEDS), BF16),
            pltpu.VMEM((1024, 512), BF16),
            pltpu.SemaphoreType.DMA((TIMES - 1,)),
        ],
        compiler_params=params(42),
        cost_estimate=cost(1280, 4 << 20),
        name="second_time",
    )(voltages, first, gains, table, window)
    power_23, keep = pl.pallas_call(
        later_kernel,
        in_specs=[VMEM] * 5,
        out_specs=[VMEM] * 2,
        out_shape=[powers_of(TIMES - 2), jax.ShapeDtypeStruct((2, PAST, FEEDS), BF16)],
        scratch_shapes=[pltpu.VMEM((1024, 512), BF16)],
        compiler_params=params(24),
        cost_estimate=cost(2048, 4 << 20),
        name="later_times",
    )(blocks, second, gains, table, bank)
    returned = pl.pallas_call(
        neighbour_kernel,
        in_specs=[VMEM] * 5,
        out_specs=VMEM,
        out_shape=jax.ShapeDtypeStruct((EW, 2, FINE, NS // 2), BF16),
        scratch_shapes=[pltpu.VMEM((192, 512), BF16)],
        compiler_params=params(16),
        cost_estimate=cost(192, 1 << 20),
        name="next_block",
    )(head, keep, gains, table, bank)
    returned = lax.ppermute(returned, "tm", forward)
    power = pl.pallas_call(
        first_kernel,
        in_specs=[VMEM] * 9,
        out_specs=VMEM,
        out_shape=powers_of(TIMES),
        scratch_shapes=[pltpu.VMEM((576, 512), BF16)],
        compiler_params=params(24),
        cost_estimate=cost(576, 3 << 20),
        name="first_time",
    )(halo, first, returned, late, gains, table, bank, power_1, power_23)
    got = lax.all_to_all(power, "freq", split_axis=0, concat_axis=0, tiled=True)
    chunks = 8
    wide = GROUP * CHAN * FINE
    joined = pl.pallas_call(
        join_kernel,
        in_specs=[VMEM],
        out_specs=HBM,
        out_shape=jax.ShapeDtypeStruct((HALF, 2, TIMES, wide), F32),
        scratch_shapes=[
            pltpu.VMEM((chunks, HALF, 2, TIMES, wide // chunks), F32),
            pltpu.SemaphoreType.DMA((chunks,)),
        ],
        compiler_params=params(16),
        name="join_channels",
    )(got)
    return joined.reshape(GROUP, TIMES, wide)


def solution(mesh):
    placed = (P(None, "tm", "freq", None), P(None, "freq", None), P())
    return jax.shard_map(
        body, mesh=mesh, in_specs=placed, out_specs=P("freq", "tm", None), check_vma=False
    )
```
